32 devices in a mesh: parts: 2 (over x), seq: 8 (over z, y), head: 2 (over core).
Axes of the slice: x: 2, y: 2, z: 4, core: 2. Of those that a mesh axis runs over, the one named last changes fastest.
Arguments:
- queries: bfloat16 [8192, 2048], P(('parts', 'seq', 'head')), parts along dimension 0, may hold values from -6 to 6
- keys: bfloat16 [8192, 2048], P(('parts', 'seq', 'head')), parts along dimension 0, may hold values from -6 to 6
- values: bfloat16 [8192, 2048], P(('parts', 'seq', 'head')), parts along dimension 0, may hold values from -25 to 25
- out_grad: bfloat16 [8192, 2048], P(('parts', 'seq', 'head')), parts along dimension 0, may hold values from -6 to 6
- log_decay: bfloat16 [8192, 16], P(('parts', 'seq', 'head')), parts along dimension 0, may hold values from -1.6 to 0, as said below
Outputs:
- out: bfloat16 [8192, 2048], P(('parts', 'seq', 'head')), parts along dimension 0
- query_grad: bfloat16 [8192, 2048], P(('parts', 'seq', 'head')), parts along dimension 0
- key_grad: bfloat16 [8192, 2048], P(('parts', 'seq', 'head')), parts along dimension 0
- value_grad: bfloat16 [8192, 2048], P(('parts', 'seq', 'head')), parts along dimension 0
The draws below stay inside these ranges and needn't reach their ends.
There are 2 independent parts, one for each index of `parts`. The reference program is written for one: setup_inputs(seed, part) draws one part's arguments, and reference() takes and returns one part's arrays. A program takes and returns all parts, laid end to end along the dimension named above; each array names one. Nothing has to cross between parts.
Inputs may be any that keep to these rules, and one draw needn't show every extreme that they name: `log_decay`: strictly negative.
All inputs are finite; a program needn't handle non-finite values.
Results may differ from the reference program's by a relative error of at most 0.0053.
Values may be sent and summed in bfloat16 or wider, within the bound.
A program may use at most 128 MiB of HBM per device.

```python
import math
import jax
import jax.numpy as jnp
from jax import lax

H = 16
DH = 128
TOK_DEV = 256
BLOCK = 256
TOKENS = 4096


def draw_log_decay(key, part):
    key = jax.random.fold_in(key, 11)
    keys_all = jax.random.split(key, 6)
    fast_share = 0.5
    fast = jax.random.bernoulli(keys_all[0], fast_share, (H,))
    fast_rate = jnp.exp(jax.random.uniform(keys_all[1], (H,), jnp.float32, math.log(1.0 / 50.0), math.log(1.0 / 30.0)))
    slow_rate = 0.2 / TOKENS * jnp.exp(jax.random.uniform(keys_all[2], (H,), jnp.float32, math.log(0.5), 0.0))
    base = jnp.where(fast, fast_rate, slow_rate)
    groups = TOKENS // TOK_DEV
    factor = jnp.exp(jax.random.uniform(keys_all[3], (groups, 1), jnp.float32, math.log(0.7), math.log(1.4)))
    decay_speed = jnp.repeat(factor, TOK_DEV, axis=0) * base[None, :]
    spots = jax.random.randint(keys_all[4], (3,), 0, TOKENS)
    retain_factor = jax.random.uniform(keys_all[5], (3,), jnp.float32, 0.6, 0.8)
    positions = jnp.arange(TOKENS)
    dropped_entries = positions[:, None] == spots[None, :]
    spike_amount = jnp.sum(jnp.where(dropped_entries, -jnp.log(retain_factor)[None, :], 0.0), axis=1)
    return (-(decay_speed + spike_amount[:, None])).astype(jnp.bfloat16)


def draw_values(key, part):
    key = jax.random.fold_in(key, 29)
    keys_all = jax.random.split(key, 3)
    columns = jnp.exp(jax.random.uniform(keys_all[0], (H * DH,), jnp.float32, math.log(0.3), math.log(3.0)))
    base = jnp.clip(jax.random.normal(keys_all[1], (TOKENS, H * DH), jnp.float32), -4.0, 4.0)
    rowscale = jnp.exp(jax.random.uniform(keys_all[2], (TOKENS, 1), jnp.float32, math.log(0.6), math.log(1.6)))
    mixed = rowscale * base
    return (mixed * columns[None, :]).astype(jnp.bfloat16)


def shard_levels(rng, dims, pieces, low, high):
    factor_of, own = 1.0, jax.random.fold_in(rng, 6)
    for position, blocks in pieces:
        heights = jnp.exp(jax.random.uniform(jax.random.fold_in(own, position), (blocks,), jnp.float32, low / len(pieces), high / len(pieces)))
        factor_of = factor_of * jnp.repeat(heights, dims[position] // blocks).reshape([-1 if axis == position else 1 for axis in range(len(dims))])
    return factor_of


def normal_values(own_key, shape, width, bound, shards=(), held_as=jnp.bfloat16):
    entries = jax.random.normal(own_key, shape, jnp.float32) * width
    if len(shards) > 0:
        entries = shard_levels(own_key, shape, shards, -0.22, 0.18) * entries
    return jnp.clip(entries, min=-bound, max=bound).astype(held_as)


def setup_inputs(seed: int = 0, part: int = 0) -> dict:
    key_list = jax.random.split(jax.random.key(seed), 6)
    part_keys = jax.random.split(jax.random.fold_in(key_list[5], part), 6)
    return {
        "queries": normal_values(part_keys[0], (TOKENS, H * DH), 1.0, 6.0, ((0, 16),)),
        "keys": normal_values(part_keys[1], (TOKENS, H * DH), 1.0, 6.0, ((0, 16),)),
        "values": draw_values(jax.random.fold_in(jax.random.fold_in(key_list[5], part), 71), part),
        "out_grad": normal_values(part_keys[3], (TOKENS, H * DH), 1.0, 6.0, ((0, 16),)),
        "log_decay": draw_log_decay(jax.random.fold_in(jax.random.fold_in(key_list[5], part), 71), part),
    }


EPSILON = 1e-06
highest = lax.Precision.HIGHEST

def decay_weights(within_b):
    size = within_b.shape[0]
    index = jnp.arange(size)
    lower = index[:, None] >= index[None, :]
    spread = within_b.T[:, :, None] - within_b.T[:, None, :]
    return jnp.where(lower[None], jnp.exp(jnp.minimum(spread, 0.0)), 0.0)

def block_scores(query_b, key_b, within_b):
    weights = decay_weights(within_b)
    scores = jnp.einsum('thd,shd->hts', query_b.astype(jnp.float32), key_b.astype(jnp.float32)) * weights
    return (weights, scores)

def reference(queries, keys, values, out_grad, log_decay):
    blocks = TOKENS // BLOCK
    shape4 = (blocks, BLOCK, H, DH)
    query_blocks = queries.reshape(shape4)
    key_blocks = keys.reshape(shape4)
    value_blocks = values.reshape(shape4)
    cotan_blocks = out_grad.reshape(shape4)
    within = jnp.cumsum(log_decay.astype(jnp.float32).reshape(blocks, BLOCK, H), axis=1)
    blank = jnp.zeros((H, DH, DH), jnp.float32)

    def forward_step(enter, piece):
        query_b, key_b, value_b, cotan_b, within_b = piece
        total = within_b[-1]
        weights, scores = block_scores(query_b, key_b, within_b)
        scores_b = lax.optimization_barrier(scores.astype(jnp.bfloat16)).astype(jnp.float32)
        query_wide = query_b.astype(jnp.float32)
        value_wide = value_b.astype(jnp.float32)
        cross = jnp.einsum('thd,hde->the', query_wide, enter, precision=highest)
        numer = jnp.einsum('hts,she->the', scores_b, value_wide) + jnp.exp(within_b)[:, :, None] * cross
        scale = jnp.sqrt(lax.optimization_barrier(jnp.mean(numer * numer, axis=-1, keepdims=True)) + EPSILON)
        normed = numer / scale
        cotan = cotan_b.astype(jnp.float32)
        grad_num = (cotan - normed * lax.optimization_barrier(jnp.mean(cotan * normed, axis=-1, keepdims=True))) / scale
        fading = jnp.exp(total[None, :] - within_b)
        local = jnp.einsum('shd,she->hde', key_b.astype(jnp.float32) * fading[:, :, None], value_wide, precision=highest)
        hterm = jnp.einsum('thd,the->hde', query_wide * jnp.exp(within_b)[:, :, None], grad_num, precision=highest)
        leave = jnp.exp(total)[:, None, None] * enter + local
        return (leave, (enter, normed.astype(jnp.bfloat16), grad_num, hterm))
    discarded_state, (enters, outputs, grads, hterms) = lax.scan(forward_step, blank, (query_blocks, key_blocks, value_blocks, cotan_blocks, within))

    def backward_step(back, piece):
        query_b, key_b, value_b, within_b, enter, grad_num, hterm = piece
        total = within_b[-1]
        weights, scores = block_scores(query_b, key_b, within_b)
        scores_b = lax.optimization_barrier(scores.astype(jnp.bfloat16)).astype(jnp.float32)
        grad_short = lax.optimization_barrier(grad_num.astype(jnp.bfloat16)).astype(jnp.float32)
        query_wide = query_b.astype(jnp.float32)
        key_wide = key_b.astype(jnp.float32)
        value_wide = value_b.astype(jnp.float32)
        mixed = jnp.einsum('the,she->hts', grad_short, value_wide) * weights
        mixed_b = lax.optimization_barrier(mixed.astype(jnp.bfloat16)).astype(jnp.float32)
        fading = jnp.exp(total[None, :] - within_b)[:, :, None]
        query_grad = jnp.einsum('hts,shd->thd', mixed_b, key_wide) + jnp.exp(within_b)[:, :, None] * jnp.einsum('the,hde->thd', grad_num, enter, precision=highest)
        key_grad = jnp.einsum('hts,thd->shd', mixed_b, query_wide) + fading * jnp.einsum('she,hde->shd', value_wide, back, precision=highest)
        value_grad = jnp.einsum('hts,the->she', scores_b, grad_short) + fading * jnp.einsum('shd,hde->she', key_wide, back, precision=highest)
        earlier = jnp.exp(total)[:, None, None] * back + hterm
        return (earlier, (query_grad.astype(jnp.bfloat16), key_grad.astype(jnp.bfloat16), value_grad.astype(jnp.bfloat16)))
    unused_grad, (query_grads, key_grads, value_grads) = lax.scan(backward_step, blank, (query_blocks, key_blocks, value_blocks, within, enters, grads, hterms), reverse=True)
    flat = (TOKENS, H * DH)
    return (outputs.reshape(flat), query_grads.reshape(flat), key_grads.reshape(flat), value_grads.reshape(flat))
```

```python
import functools

import jax
import jax.numpy as jnp
from jax import lax
from jax.experimental import pallas as pl
from jax.experimental.pallas import tpu as pltpu
from jax.sharding import PartitionSpec as P

DH = 128
EPSILON = 1e-06
CHUNKS = 4
F32 = jnp.float32
BF16 = jnp.bfloat16
MESH = pl.DeviceIdType.MESH


def dot(a, b, contract):
    return lax.dot_general(a, b, ((contract[0], contract[1]), ((), ())), preferred_element_type=F32)


NN = ((1,), (0,))
NT = ((1,), (1,))
TN = ((0,), (0,))


def kernel(
    groups, heads, q_hbm, k_hbm, v_hbm, g_hbm, ld_ref, o_hbm, dq_hbm, dk_hbm, dv_hbm,
    q, k, v, g, o, dq, dk, dv, colb, wrow, bias, wgt, sb, intra, gs, kpart,
    st, cc, tt, m1s, m1r, m2s, m2r, m3s, m3r, m4s, ent,
    in_sem, out_sem, ss, rs, ts, tr,
):
    rows = q.shape[0]
    half = heads // 2
    per = half // CHUNKS
    wire = m1s.dtype
    seq = lax.axis_index("seq")
    c = lax.axis_index("head")
    group = seq // 2
    y = seq - 2 * group
    twin = 2 * group + (1 - y)
    partner = {"head": 1 - c}
    peers = (partner, {"seq": twin}, {"seq": twin, "head": 1 - c})
    has_before = group > 0
    has_after = group < groups - 1

    loads = [
        pltpu.make_async_copy(a, b, in_sem.at[i])
        for i, (a, b) in enumerate(((k_hbm, k), (v_hbm, v), (q_hbm, q), (g_hbm, g)))
    ]
    for load in loads:
        load.start()

    barrier = pltpu.get_barrier_semaphore()
    for peer in peers:
        pl.semaphore_signal(barrier, inc=1, device_id=peer, device_id_type=MESH)

    @pl.when(has_before)
    def _():
        pl.semaphore_signal(barrier, inc=1, device_id={"seq": seq - 2}, device_id_type=MESH)

    @pl.when(has_after)
    def _():
        pl.semaphore_signal(barrier, inc=1, device_id={"seq": seq + 2}, device_id_type=MESH)

    def cols(h):
        return pl.ds(pl.multiple_of(h * DH, DH), DH)

    row_i = lax.broadcasted_iota(jnp.int32, (rows, rows), 0)
    col_i = lax.broadcasted_iota(jnp.int32, (rows, rows), 1)
    lower = row_i >= col_i
    bias[...] = jnp.where(lower, 0.0, -1e30)
    tri = jnp.where(lower, 1.0, 0.0).astype(BF16)
    ld = ld_ref[...]
    within = dot(tri, ld, NN)
    wrow[...] = dot(ld, tri, ((0,), (1,)))
    for h in range(heads):
        spread = jnp.broadcast_to(within[:, h : h + 1], (rows, DH))
        colb[h] = spread
        tt[0, h : h + 1, :] = spread[rows - 1 : rows, :]

    pl.semaphore_wait(barrier, 3 + has_before.astype(jnp.int32) + has_after.astype(jnp.int32))

    def total_copy(i):
        return pltpu.make_async_remote_copy(
            src_ref=tt.at[0], dst_ref=tt.at[i + 1], send_sem=ts.at[i], recv_sem=tr.at[i],
            device_id=peers[i], device_id_type=MESH,
        )

    for i in range(3):
        total_copy(i).start()

    def remote(kind, d, ch, src, dst, peer):
        return pltpu.make_async_remote_copy(
            src_ref=src, dst_ref=dst, send_sem=ss.at[kind, d, ch], recv_sem=rs.at[kind, d, ch],
            device_id=peer, device_id_type=MESH,
        )

    def move1(d, ch):
        part = pl.ds(ch * per, per)
        return remote(0, d, ch, m1s.at[d, part], m1r.at[d, part], partner)

    def move2(d, ch):
        part = pl.ds(ch * per, per)
        return remote(1, d, ch, m2s.at[d, part], m2r.at[d, part], {"seq": twin})

    def move3(d, ch):
        part = pl.ds(ch * per, per)
        step = 2 if d == 0 else -2
        return remote(2, d, ch, m3s.at[d, part], m3r.at[d, part], {"seq": seq + step})

    def move4(d, ch, base):
        part = pl.ds(ch * per, per)
        return remote(3, d, ch, m4s.at[d, part], ent.at[d, pl.ds(base * half + ch * per, per)], partner)

    def chunked(body):
        lax.fori_loop(0, CHUNKS, lambda ch, _: (body(ch), 0)[1], 0)

    def each(count, body):
        lax.fori_loop(0, count, lambda i, _: (body(i), 0)[1], 0)

    def total(rel, h):
        return tt[rel, pl.ds(h, 1), :]

    def combine_cores(d, ch):
        move1(d, ch).wait_recv()
        first = (c if d == 0 else 1 - c) == 0
        for i in range(per):
            j = ch * per + i
            h = c * half + j
            mine, other = st[d, j], m1r[d, j].astype(F32)
            fade_mine = jnp.where(first, jnp.exp(total(1, h)), 1.0)
            fade_other = jnp.where(first, 1.0, jnp.exp(total(0, h)))
            both = fade_mine * mine + fade_other * other
            cc[j] = both
            m2s[d, j] = both.astype(wire)
        move2(d, ch).start()

    def chain(d, ch):
        has_in = has_before if d == 0 else has_after
        has_out = has_after if d == 0 else has_before
        first = (c if d == 0 else 1 - c) == 0
        first_chip = (y if d == 0 else 1 - y) == 0
        move2(d, ch).wait_recv()

        @pl.when(has_in)
        def _():
            move3(d, ch).wait_recv()

        @pl.when(has_out)
        def _():
            for i in range(per):
                j = ch * per + i
                h = c * half + j
                t_mine = total(0, h) + total(1, h)
                t_other = total(2, h) + total(3, h)
                fade_mine = jnp.where(first_chip, jnp.exp(t_other), 1.0)
                fade_other = jnp.where(first_chip, 1.0, jnp.exp(t_mine))
                whole = fade_mine * cc[j] + fade_other * m2r[d, j].astype(F32)
                m3s[d, j] = (jnp.exp(t_mine + t_other) * m3r[d, j].astype(F32) + whole).astype(wire)
            move3(d, ch).start()

        for i in range(per):
            j = ch * per + i
            h = c * half + j
            t_other = total(2, h) + total(3, h)
            fade_in = jnp.where(first_chip, 1.0, jnp.exp(t_other))
            add_in = jnp.where(first_chip, 0.0, 1.0)
            chip_in = fade_in * m3r[d, j].astype(F32) + add_in * m2r[d, j].astype(F32)
            t_first = jnp.where(first, total(0, h), total(1, h))
            state_first = jnp.where(first, st[d, j], m1r[d, j].astype(F32))
            later = jnp.exp(t_first) * chip_in + state_first
            ent[d, h] = jnp.where(first, chip_in, later).astype(wire)
            m4s[d, j] = jnp.where(first, later, chip_in).astype(wire)
        move4(d, ch, c).start()

    @pl.when(jnp.logical_not(has_before))
    def _():
        m3r[0] = jnp.zeros(m3r.shape[1:], wire)

    @pl.when(jnp.logical_not(has_after))
    def _():
        m3r[1] = jnp.zeros(m3r.shape[1:], wire)

    loads[0].wait()
    loads[1].wait()

    def local_state(h):
        fading = jnp.exp(total(0, h) - colb[h])
        faded = (k[:, cols(h)].astype(F32) * fading).astype(BF16)
        return dot(faded, v[:, cols(h)], TN)

    def send_local(ch):
        for i in range(per):
            j = ch * per + i
            m1s[0, j] = local_state((1 - c) * half + j).astype(wire)
        move1(0, ch).start()

    chunked(send_local)

    def keep_local(ch):
        for i in range(per):
            j = ch * per + i
            st[0, j] = local_state(c * half + j)

    chunked(keep_local)
    loads[2].wait()

    def inside(h):
        column = colb[h]
        spread = jnp.concatenate([column, column], axis=1) - wrow[pl.ds(h, 1), :]
        weights = jnp.exp(jnp.minimum(spread, bias[...]))
        wgt[h] = weights
        scores = (dot(q[:, cols(h)], k[:, cols(h)], NT) * weights).astype(BF16)
        sb[h] = scores
        intra[h] = dot(scores, v[:, cols(h)], NN)

    def inside_own(i):
        inside(c * half + 2 * i)
        inside(c * half + 2 * i + 1)

    def inside_partner(i):
        inside((1 - c) * half + 2 * i)
        inside((1 - c) * half + 2 * i + 1)

    each(half // 4, inside_own)
    for i in range(3):
        total_copy(i).wait_recv()
    chunked(lambda ch: combine_cores(0, ch))
    lax.fori_loop(half // 4, half // 2, lambda i, _: (inside_own(i), 0)[1], 0)
    chunked(lambda ch: chain(0, ch))
    each(half // 2, inside_partner)
    loads[3].wait()

    def normalize(h):
        growing = jnp.exp(colb[h])
        q_h = q[:, cols(h)]
        numer = intra[h] + growing * dot(q_h, ent[0, h].astype(BF16), NN)
        inv = lax.rsqrt(jnp.mean(numer * numer, axis=-1, keepdims=True) + EPSILON)
        normed = numer * inv
        o[:, cols(h)] = normed.astype(BF16)
        g_h = g[:, cols(h)].astype(F32)
        grad = (g_h - normed * jnp.mean(g_h * normed, axis=-1, keepdims=True)) * inv
        short = grad.astype(BF16)
        gs[h] = short
        grown = (q_h.astype(F32) * growing).astype(BF16)
        return dot(grown, short, TN)

    def normalize_own(ch):
        for i in range(per):
            j = ch * per + i
            st[1, j] = normalize(c * half + j)

    def normalize_partner(ch):
        move4(0, ch, 1 - c).wait_recv()
        for i in range(per):
            j = ch * per + i
            m1s[1, j] = normalize((1 - c) * half + j).astype(wire)
        move1(1, ch).start()

    chunked(normalize_own)
    chunked(normalize_partner)
    out_copies = [
        pltpu.make_async_copy(a, b, out_sem.at[i])
        for i, (a, b) in enumerate(((o, o_hbm), (dq, dq_hbm), (dk, dk_hbm), (dv, dv_hbm)))
    ]
    out_copies[0].start()

    def gradients(h):
        short = gs[h]
        k_h = k[:, cols(h)]
        mixed = (dot(short, v[:, cols(h)], NT) * wgt[h]).astype(BF16)
        cross = dot(short, ent[0, h].astype(BF16), NT)
        dq[:, cols(h)] = (dot(mixed, k_h, NN) + jnp.exp(colb[h]) * cross).astype(BF16)
        kpart[h] = dot(mixed, q[:, cols(h)], TN)
        intra[h] = dot(sb[h], short, TN)

    def gradients_own(i):
        gradients(c * half + 2 * i)
        gradients(c * half + 2 * i + 1)

    def gradients_partner(i):
        gradients((1 - c) * half + 2 * i)
        gradients((1 - c) * half + 2 * i + 1)

    each(half // 4, gradients_own)
    chunked(lambda ch: combine_cores(1, ch))
    lax.fori_loop(half // 4, half // 2, lambda i, _: (gradients_own(i), 0)[1], 0)
    chunked(lambda ch: chain(1, ch))
    each(half // 2, gradients_partner)
    out_copies[1].start()

    def finish(h):
        fading = jnp.exp(total(0, h) - colb[h])
        back = ent[1, h].astype(BF16)
        dk[:, cols(h)] = (kpart[h] + fading * dot(v[:, cols(h)], back, NT)).astype(BF16)
        dv[:, cols(h)] = (intra[h] + fading * dot(k[:, cols(h)], back, NN)).astype(BF16)

    def finish_own(ch):
        for i in range(per):
            finish(c * half + ch * per + i)

    def finish_partner(ch):
        move4(1, ch, 1 - c).wait_recv()
        for i in range(per):
            finish((1 - c) * half + ch * per + i)

    chunked(finish_own)
    chunked(finish_partner)
    out_copies[2].start()
    out_copies[3].start()

    for i in range(3):
        total_copy(i).wait_send()
    for d in range(2):

        def drain(ch, d=d):
            move1(d, ch).wait_send()
            move2(d, ch).wait_send()
            move4(d, ch, c).wait_send()

            @pl.when(has_after if d == 0 else has_before)
            def _():
                move3(d, ch).wait_send()

        chunked(drain)
    for copy in out_copies:
        copy.wait()


def body(groups, queries, keys, values, out_grad, log_decay):
    rows, width = queries.shape
    heads = width // DH
    half = heads // 2
    wire = BF16 if groups <= 8 else F32
    array = jax.ShapeDtypeStruct((rows, width), BF16)
    any_spec = pl.BlockSpec(memory_space=pl.ANY)
    moved = pltpu.VMEM((2, half, DH, DH), wire)
    return pl.pallas_call(
        functools.partial(kernel, groups, heads),
        out_shape=(array,) * 4,
        in_specs=[any_spec] * 4 + [pl.BlockSpec(memory_space=pltpu.VMEM)],
        out_specs=(any_spec,) * 4,
        scratch_shapes=[pltpu.VMEM((rows, width), BF16)] * 8
        + [
            pltpu.VMEM((heads, rows, DH), F32),
            pltpu.VMEM((heads, rows), F32),
            pltpu.VMEM((rows, rows), F32),
            pltpu.VMEM((heads, rows, rows), F32),
            pltpu.VMEM((heads, rows, rows), BF16),
            pltpu.VMEM((heads, rows, DH), F32),
            pltpu.VMEM((heads, rows, DH), BF16),
            pltpu.VMEM((heads, rows, DH), F32),
            pltpu.VMEM((2, half, DH, DH), F32),
            pltpu.VMEM((half, DH, DH), F32),
            pltpu.VMEM((4, heads, DH), F32),
        ]
        + [moved] * 7
        + [
            pltpu.VMEM((2, heads, DH, DH), wire),
            pltpu.SemaphoreType.DMA((4,)),
            pltpu.SemaphoreType.DMA((4,)),
            pltpu.SemaphoreType.DMA((4, 2, CHUNKS)),
            pltpu.SemaphoreType.DMA((4, 2, CHUNKS)),
            pltpu.SemaphoreType.DMA((3,)),
            pltpu.SemaphoreType.DMA((3,)),
        ],
        compiler_params=pltpu.CompilerParams(
            collective_id=0, has_side_effects=True, vmem_limit_bytes=52 * 1024 * 1024
        ),
    )(queries, keys, values, out_grad, log_decay)


def solution(mesh):
    placed = P(("parts", "seq", "head"), None)
    return jax.shard_map(
        functools.partial(body, mesh.shape["seq"] // 2),
        mesh=mesh,
        in_specs=(placed,) * 5,
        out_specs=(placed,) * 4,
        check_vma=False,
    )
```

```python
import functools

import jax
import jax.numpy as jnp
from jax import lax
from jax.experimental import pallas as pl
from jax.experimental.pallas import tpu as pltpu
from jax.sharding import PartitionSpec as P

DH = 128
EPSILON = 1e-06
CHUNKS = 4
F32 = jnp.float32
BF16 = jnp.bfloat16
MESH = pl.DeviceIdType.MESH


def dot(a, b, contract):
    return lax.dot_general(a, b, ((contract[0], contract[1]), ((), ())), preferred_element_type=F32)


def lane_mean(a):
    high = a.astype(BF16)
    low = (a - high.astype(F32)).astype(BF16)
    share = jnp.full((2 * DH, DH), 1.0 / DH, BF16)
    return dot(jnp.concatenate([high, low], axis=1), share, NN)


NN = ((1,), (0,))
NT = ((1,), (1,))
TN = ((0,), (0,))


def kernel(
    groups, heads, q_hbm, k_hbm, v_hbm, g_hbm, ld_hbm, o, dq, dk, dv,
    q, k, v, g, ld_ref, colb, wrow, bias, wgt, sb, intra, gs, kpart,
    st, cc, tt, m1s, m1r, m2s, m2r, m3s, m3r, m4s, ent,
    in_sem, ss, rs, ts, tr,
):
    rows = q.shape[0]
    half = heads // 2
    per = half // CHUNKS
    wire = m1s.dtype
    seq = lax.axis_index("seq")
    c = lax.axis_index("head")
    group = seq // 2
    y = seq - 2 * group
    twin = 2 * group + (1 - y)
    partner = {"head": 1 - c}
    peers = (partner, {"seq": twin}, {"seq": twin, "head": 1 - c})
    has_before = group > 0
    has_after = group < groups - 1

    loads = [
        pltpu.make_async_copy(a, b, in_sem.at[i])
        for i, (a, b) in enumerate(
            ((k_hbm, k), (v_hbm, v), (q_hbm, q), (g_hbm, g), (ld_hbm, ld_ref))
        )
    ]
    for i in (4, 0, 1, 2, 3):
        loads[i].start()

    barrier = pltpu.get_barrier_semaphore()
    for peer in peers:
        pl.semaphore_signal(barrier, inc=1, device_id=peer, device_id_type=MESH)

    @pl.when(has_before)
    def _():
        pl.semaphore_signal(barrier, inc=1, device_id={"seq": seq - 2}, device_id_type=MESH)

    @pl.when(has_after)
    def _():
        pl.semaphore_signal(barrier, inc=1, device_id={"seq": seq + 2}, device_id_type=MESH)

    def cols(h):
        return pl.ds(pl.multiple_of(h * DH, DH), DH)

    row_i = lax.broadcasted_iota(jnp.int32, (rows, rows), 0)
    col_i = lax.broadcasted_iota(jnp.int32, (rows, rows), 1)
    lower = row_i >= col_i
    bias[...] = jnp.where(lower, 0.0, -1e30)
    tri = jnp.where(lower, 1.0, 0.0).astype(BF16)
    loads[4].wait()
    ld = ld_ref[...]
    within = dot(tri, ld, NN)
    wrow[...] = dot(ld, tri, ((0,), (1,)))
    for h in range(heads):
        spread = jnp.broadcast_to(within[:, h : h + 1], (rows, DH))
        colb[h] = spread
        tt[0, h : h + 1, :] = spread[rows - 1 : rows, :]

    pl.semaphore_wait(barrier, 3 + has_before.astype(jnp.int32) + has_after.astype(jnp.int32))

    def total_copy(i):
        return pltpu.make_async_remote_copy(
            src_ref=tt.at[0], dst_ref=tt.at[i + 1], send_sem=ts.at[i], recv_sem=tr.at[i],
            device_id=peers[i], device_id_type=MESH,
        )

    for i in range(3):
        total_copy(i).start()

    def remote(kind, d, ch, src, dst, peer):
        return pltpu.make_async_remote_copy(
            src_ref=src, dst_ref=dst, send_sem=ss.at[kind, d, ch], recv_sem=rs.at[kind, d, ch],
            device_id=peer, device_id_type=MESH,
        )

    def move1(d, ch):
        part = pl.ds(ch * per, per)
        return remote(0, d, ch, m1s.at[d, part], m1r.at[d, part], partner)

    def move2(d, ch):
        part = pl.ds(ch * per, per)
        return remote(1, d, ch, m2s.at[d, part], m2r.at[d, part], {"seq": twin})

    def move3(d, j):
        part = pl.ds(j, 1)
        step = 2 if d == 0 else -2
        return remote(2, d, j, m3s.at[d, part], m3r.at[d, part], {"seq": seq + step})

    def move4(d, ch, base):
        part = pl.ds(ch * per, per)
        return remote(3, d, ch, m4s.at[d, part], ent.at[d, pl.ds(base * half + ch * per, per)], partner)

    def chunked(body):
        lax.fori_loop(0, CHUNKS, lambda ch, _: (body(ch), 0)[1], 0)

    def span(start, stop, body):
        lax.fori_loop(start, stop, lambda i, _: (body(i), 0)[1], 0)

    def total(rel, h):
        return tt[rel, pl.ds(h, 1), :]

    def combine_cores(d, ch):
        move1(d, ch).wait_recv()
        first = (c if d == 0 else 1 - c) == 0
        for i in range(per):
            j = ch * per + i
            h = c * half + j
            mine, other = st[d, j], m1r[d, j].astype(F32)
            fade_mine = jnp.where(first, jnp.exp(total(1, h)), 1.0)
            fade_other = jnp.where(first, 1.0, jnp.exp(total(0, h)))
            both = fade_mine * mine + fade_other * other
            cc[j] = both
            m2s[d, j] = both.astype(wire)
        move2(d, ch).start()

    def relay(d, ch):
        has_in = has_before if d == 0 else has_after
        has_out = has_after if d == 0 else has_before
        first_chip = (y if d == 0 else 1 - y) == 0
        move2(d, ch).wait_recv()
        for i in range(per):
            j = ch * per + i
            h = c * half + j
            t_mine = total(0, h) + total(1, h)
            t_other = total(2, h) + total(3, h)
            fade_mine = jnp.where(first_chip, jnp.exp(t_other), 1.0)
            fade_other = jnp.where(first_chip, 1.0, jnp.exp(t_mine))
            fade_all = jnp.exp(t_mine + t_other)
            whole = fade_mine * cc[j] + fade_other * m2r[d, j].astype(F32)

            @pl.when(has_in)
            def _():
                move3(d, j).wait_recv()

            @pl.when(has_out)
            def _():
                m3s[d, j] = (fade_all * m3r[d, j].astype(F32) + whole).astype(wire)
                move3(d, j).start()

    def enter(d, ch):
        first = (c if d == 0 else 1 - c) == 0
        first_chip = (y if d == 0 else 1 - y) == 0
        for i in range(per):
            j = ch * per + i
            h = c * half + j
            t_other = total(2, h) + total(3, h)
            fade_in = jnp.where(first_chip, 1.0, jnp.exp(t_other))
            add_in = jnp.where(first_chip, 0.0, 1.0)
            chip_in = fade_in * m3r[d, j].astype(F32) + add_in * m2r[d, j].astype(F32)
            t_first = jnp.where(first, total(0, h), total(1, h))
            state_first = jnp.where(first, st[d, j], m1r[d, j].astype(F32))
            later = jnp.exp(t_first) * chip_in + state_first
            ent[d, h] = jnp.where(first, chip_in, later).astype(wire)
            m4s[d, j] = jnp.where(first, later, chip_in).astype(wire)
        move4(d, ch, c).start()

    def relay_all(d, has_out):
        @pl.when(has_out)
        def _():
            chunked(lambda ch: relay(d, ch))

    def arrive(d, ch, has_out):
        @pl.when(jnp.logical_not(has_out))
        def _():
            relay(d, ch)

        enter(d, ch)

    @pl.when(jnp.logical_not(has_before))
    def _():
        m3r[0] = jnp.zeros(m3r.shape[1:], wire)

    @pl.when(jnp.logical_not(has_after))
    def _():
        m3r[1] = jnp.zeros(m3r.shape[1:], wire)

    loads[0].wait()
    loads[1].wait()

    def local_state(h):
        fading = jnp.exp(total(0, h) - colb[h])
        faded = (k[:, cols(h)].astype(F32) * fading).astype(BF16)
        return dot(faded, v[:, cols(h)], TN)

    def send_local(ch):
        for i in range(per):
            j = ch * per + i
            m1s[0, j] = local_state((1 - c) * half + j).astype(wire)
        move1(0, ch).start()

    chunked(send_local)

    def keep_local(ch):
        for i in range(per):
            j = ch * per + i
            st[0, j] = local_state(c * half + j)

    chunked(keep_local)
    loads[2].wait()

    def inside(h):
        column = colb[h]
        spread = jnp.concatenate([column, column], axis=1) - wrow[pl.ds(h, 1), :]
        weights = jnp.exp(jnp.minimum(spread, bias[...]))
        wgt[h] = weights
        scores = (dot(q[:, cols(h)], k[:, cols(h)], NT) * weights).astype(BF16)
        sb[h] = scores
        intra[h] = dot(scores, v[:, cols(h)], NN)

    def inside_pair(i):
        inside(2 * i)
        inside(2 * i + 1)

    for i in range(3):
        total_copy(i).wait_recv()
    chunked(lambda ch: combine_cores(0, ch))
    early = jnp.where(has_before, half, 2)
    span(0, early, inside_pair)
    relay_all(0, has_after)
    span(early, half, inside_pair)
    loads[3].wait()

    def normalize(h):
        growing = jnp.exp(colb[h])
        q_h = q[:, cols(h)]
        numer = intra[h] + growing * dot(q_h, ent[0, h].astype(BF16), NN)
        g_h = g[:, cols(h)].astype(F32)
        square = lane_mean(numer * numer)
        along = lane_mean(g_h * numer)
        inv = lax.rsqrt(square + EPSILON)
        normed = numer * inv
        o[:, cols(h)] = normed.astype(BF16)
        grad = (g_h - normed * (along * inv)) * inv
        short = grad.astype(BF16)
        gs[h] = short
        grown = (q_h.astype(F32) * growing).astype(BF16)
        return dot(grown, short, TN)

    def normalize_own(ch):
        for i in range(per):
            j = ch * per + i
            st[1, j] = normalize(c * half + j)

    def normalize_partner(ch):
        move4(0, ch, 1 - c).wait_recv()
        for i in range(per):
            j = ch * per + i
            m1s[1, j] = normalize((1 - c) * half + j).astype(wire)
        move1(1, ch).start()

    def forward_step(ch):
        arrive(0, ch, has_after)
        normalize_own(ch)

    def forward_both(ch):
        forward_step(ch)
        normalize_partner(ch - 1)

        @pl.when(ch >= 2)
        def _():
            combine_cores(1, ch - 2)

    forward_step(0)
    span(1, CHUNKS, forward_both)
    normalize_partner(CHUNKS - 1)
    if CHUNKS > 1:
        combine_cores(1, CHUNKS - 2)
    combine_cores(1, CHUNKS - 1)

    def gradients(h):
        short = gs[h]
        k_h = k[:, cols(h)]
        mixed = (dot(short, v[:, cols(h)], NT) * wgt[h]).astype(BF16)
        cross = dot(short, ent[0, h].astype(BF16), NT)
        dq[:, cols(h)] = (dot(mixed, k_h, NN) + jnp.exp(colb[h]) * cross).astype(BF16)
        kpart[h] = dot(mixed, q[:, cols(h)], TN)
        intra[h] = dot(sb[h], short, TN)

    def gradients_pair(i):
        gradients(2 * i)
        gradients(2 * i + 1)

    early = jnp.where(has_after, half, 2)
    span(0, early, gradients_pair)
    relay_all(1, has_before)
    span(early, half, gradients_pair)

    def finish(h):
        fading = jnp.exp(total(0, h) - colb[h])
        back = ent[1, h].astype(BF16)
        dk[:, cols(h)] = (kpart[h] + fading * dot(v[:, cols(h)], back, NT)).astype(BF16)
        dv[:, cols(h)] = (intra[h] + fading * dot(k[:, cols(h)], back, NN)).astype(BF16)

    def finish_own(ch):
        for i in range(per):
            finish(c * half + ch * per + i)

    def finish_partner(ch):
        move4(1, ch, 1 - c).wait_recv()
        for i in range(per):
            finish((1 - c) * half + ch * per + i)

    def backward_step(ch):
        arrive(1, ch, has_before)
        finish_own(ch)

    def backward_both(ch):
        backward_step(ch)
        finish_partner(ch - 1)

    backward_step(0)
    span(1, CHUNKS, backward_both)
    finish_partner(CHUNKS - 1)

    for i in range(3):
        total_copy(i).wait_send()
    for d in range(2):

        def drain(ch, d=d):
            move1(d, ch).wait_send()
            move2(d, ch).wait_send()
            move4(d, ch, c).wait_send()

            @pl.when(has_after if d == 0 else has_before)
            def _():
                for i in range(per):
                    move3(d, ch * per + i).wait_send()

        chunked(drain)


def write_out(a0, a1, a2, a3, b0, b1, b2, b3, sem):
    copies = [
        pltpu.make_async_copy(a, b, sem.at[i])
        for i, (a, b) in enumerate(((a0, b0), (a1, b1), (a2, b2), (a3, b3)))
    ]
    for copy in copies:
        copy.start()
    for copy in copies:
        copy.wait()


def body(groups, queries, keys, values, out_grad, log_decay):
    rows, width = queries.shape
    heads = width // DH
    half = heads // 2
    wire = BF16 if groups <= 8 else F32
    array = jax.ShapeDtypeStruct((rows, width), BF16)
    any_spec = pl.BlockSpec(memory_space=pl.ANY)
    hbm_spec = pl.BlockSpec(memory_space=pltpu.HBM)
    moved = pltpu.VMEM((2, half, DH, DH), wire)
    vmem_spec = pl.BlockSpec(memory_space=pltpu.VMEM)
    results = pl.pallas_call(
        functools.partial(kernel, groups, heads),
        out_shape=(pltpu.VMEM((rows, width), BF16),) * 4,
        in_specs=[hbm_spec] * 5,
        out_specs=(vmem_spec,) * 4,
        scratch_shapes=[pltpu.VMEM((rows, width), BF16)] * 4
        + [
            pltpu.VMEM(log_decay.shape, BF16),
            pltpu.VMEM((heads, rows, DH), F32),
            pltpu.VMEM((heads, rows), F32),
            pltpu.VMEM((rows, rows), F32),
            pltpu.VMEM((heads, rows, rows), F32),
            pltpu.VMEM((heads, rows, rows), BF16),
            pltpu.VMEM((heads, rows, DH), F32),
            pltpu.VMEM((heads, rows, DH), BF16),
            pltpu.VMEM((heads, rows, DH), F32),
            pltpu.VMEM((2, half, DH, DH), F32),
            pltpu.VMEM((half, DH, DH), F32),
            pltpu.VMEM((4, heads, DH), F32),
        ]
        + [moved] * 7
        + [
            pltpu.VMEM((2, heads, DH, DH), wire),
            pltpu.SemaphoreType.DMA((5,)),
            pltpu.SemaphoreType.DMA((4, 2, half)),
            pltpu.SemaphoreType.DMA((4, 2, half)),
            pltpu.SemaphoreType.DMA((3,)),
            pltpu.SemaphoreType.DMA((3,)),
        ],
        compiler_params=pltpu.CompilerParams(
            collective_id=0, has_side_effects=True, vmem_limit_bytes=52 * 1024 * 1024
        ),
    )(queries, keys, values, out_grad, log_decay)
    return pl.pallas_call(
        write_out,
        out_shape=(array,) * 4,
        in_specs=[any_spec] * 4,
        out_specs=(hbm_spec,) * 4,
        scratch_shapes=[pltpu.SemaphoreType.DMA((4,))],
        compiler_params=pltpu.CompilerParams(vmem_limit_bytes=1024 * 1024),
    )(*results)


def solution(mesh):
    placed = P(("parts", "seq", "head"), None)
    return jax.shard_map(
        functools.partial(body, mesh.shape["seq"] // 2),
        mesh=mesh,
        in_specs=(placed,) * 5,
        out_specs=(placed,) * 4,
        check_vma=False,
    )
```
